32 devices in a mesh: section: 4 (over x, core), seq: 8 (over z, y).
Axes of the slice: x: 2, y: 2, z: 4, core: 2. Of those that a mesh axis runs over, the one named last changes fastest.
Arguments:
- activations: bfloat16 [4, 2048, 1024], P('section', 'seq'), may hold values from -54 to 54
- cotangent: bfloat16 [4, 2048, 1024], P('section', 'seq'), may hold values from -6 to 6
- input_weights: bfloat16 [4, 1024, 3072], P('section'), may hold values from -3 to 3
- output_weights: bfloat16 [4, 1024, 1024], P('section'), may hold values from -0.1875 to 0.1875
- key_blocks: int32 [16, 4], P('seq'), may hold values from 0 to 15, as said below
- block_counts: int32 [16], P('seq'), may hold values from 1 to 4, as said below
Outputs:
- forward_out: bfloat16 [4, 2048, 1024], P('section', 'seq')
- backward_out: bfloat16 [4, 2048, 1024], P('section', 'seq')
The draws below stay inside these ranges and needn't reach their ends.
Inputs may be any that keep to these rules, and one draw needn't show every extreme that they name: `key_blocks`: row b: slot 0 is b; slots 1 to block_counts[b] - 1 hold distinct blocks other than b, at most 2 blocks from b; later slots repeat b. `block_counts`: some block has 4 live slots and some has 1.
All inputs are finite; a program needn't handle non-finite values.
Results may differ from the reference program's by a relative error of at most 0.0036.
Values may be sent and summed in bfloat16 or wider, within the bound.
A program may use at most 128 MiB of HBM per device.

```python
import math
import jax
import jax.numpy as jnp
from jax import lax

D = 1024
HEADS = 8
HEAD_DIM = 128
BLOCK = 128
SLOTS = 4
REACH = 2
TOKENS = 2048
WIDTH = 1024
N_SECTION = 4


def draw_activations(key, part):
    base_key, row_key, column_key = jax.random.split(key, 3)
    shape = (N_SECTION, TOKENS, D)
    row_scale = jnp.exp(jax.random.uniform(row_key, (N_SECTION, TOKENS, 1), minval=math.log(0.3), maxval=math.log(3.0)))
    column_scale = jnp.exp(jax.random.uniform(column_key, (N_SECTION, 1, D), minval=math.log(0.3), maxval=math.log(3.0)))
    base = jnp.clip(jax.random.normal(base_key, shape), -6.0, 6.0)
    return (base * row_scale * column_scale).astype(jnp.bfloat16)


def draw_input_weights(key, part):
    base_key = jax.random.fold_in(key, 0)
    width = HEADS * HEAD_DIM
    base = jnp.clip(jax.random.normal(base_key, (N_SECTION, D, 3 * width)), -6.0, 6.0) / math.sqrt(D)
    return base.astype(jnp.bfloat16)


def neighbour_lists(key):
    order_key, count_key, full_key, single_key = jax.random.split(jax.random.fold_in(key, 11), 4)
    nblock = TOKENS // BLOCK
    offsets = jnp.concatenate([jnp.arange(-REACH, 0), jnp.arange(1, REACH + 1)]).astype(jnp.int32)
    blocks = jnp.arange(nblock, dtype=jnp.int32)
    candidates = blocks[:, None] + offsets[None, :]
    inside = (candidates >= 0) & (candidates < nblock)
    ranking = jax.random.randint(order_key, (nblock, 2 * REACH), 0, 1 << 20) * (2 * REACH) + jnp.arange(2 * REACH, dtype=jnp.int32)[None, :]
    ranking = jnp.where(inside, ranking, ranking + (1 << 26))
    ranked_order = jnp.argsort(ranking, axis=1)
    chosen = jnp.take_along_axis(candidates, ranked_order, axis=1)[:, :SLOTS - 1]
    counts = jax.random.randint(count_key, (nblock,), 1, SLOTS + 1)
    counts = jnp.minimum(counts, 1 + jnp.sum(inside.astype(jnp.int32), axis=1))
    full_block = jax.random.randint(full_key, (), REACH, nblock - REACH)
    single_block = jax.random.randint(single_key, (), 0, REACH)
    counts = jnp.where(blocks == full_block, SLOTS, counts)
    counts = jnp.where(blocks == single_block, 1, counts)
    block_lists = jnp.concatenate([blocks[:, None], chosen], axis=1)
    live_slots = jnp.arange(SLOTS, dtype=jnp.int32)[None, :] < counts[:, None]
    block_lists = jnp.where(live_slots, block_lists, blocks[:, None])
    return (block_lists.astype(jnp.int32), counts.astype(jnp.int32))


def draw_key_blocks(key, part):
    return neighbour_lists(key)[0]


def draw_block_counts(key, part):
    return neighbour_lists(key)[1]


def level_of(key, dims, shards, low, top_value):
    loudness, own = 1.0, jax.random.fold_in(key, 6)
    for dim, blocks in shards:
        heights = jnp.exp(jax.random.uniform(jax.random.fold_in(own, dim), (blocks,), jnp.float32, low / len(shards), top_value / len(shards)))
        loudness = loudness * jnp.repeat(heights, dims[dim] // blocks).reshape([-1 if axis == dim else 1 for axis in range(len(dims))])
    return loudness


def normal_values(key, dims, spread, bound, cuts=(), kind=jnp.bfloat16):
    drawn = spread * jax.random.normal(key, dims, jnp.float32)
    if cuts:
        drawn = drawn * level_of(key, dims, cuts, -0.22, 0.18)
    return jnp.clip(drawn, -bound, bound).astype(kind)


def setup_inputs(seed: int = 0) -> dict:
    seeds = jax.random.split(jax.random.key(seed), 7)
    activations = draw_activations(jax.random.fold_in(seeds[6], 71), 0)
    cotangent = normal_values(seeds[1], (N_SECTION, TOKENS, D), 1.0, 6.0, ((0, 4), (1, 8)))
    input_weights = draw_input_weights(jax.random.fold_in(seeds[6], 71), 0)
    output_weights = normal_values(seeds[3], (N_SECTION, WIDTH, D), WIDTH ** -0.5, 0.1875, ((0, 4),))
    key_blocks = draw_key_blocks(jax.random.fold_in(seeds[6], 71), 0)
    block_counts = draw_block_counts(jax.random.fold_in(seeds[6], 71), 0)
    return dict(activations=activations, cotangent=cotangent, input_weights=input_weights, output_weights=output_weights, key_blocks=key_blocks, block_counts=block_counts)


EPSILON = 1e-05

def rounded(values):
    return lax.optimization_barrier(values.astype(jnp.bfloat16)).astype(jnp.float32)

def section_layer(arrived, upstream, input_weights, output_weights, key_blocks, block_counts):
    exact = lax.Precision.HIGHEST
    nblock = key_blocks.shape[0]
    slot_count = key_blocks.shape[1]
    scaling = HEAD_DIM ** (-0.5)
    values = arrived.astype(jnp.float32)
    factor = lax.rsqrt(lax.optimization_barrier(jnp.mean(values * values, axis=-1, keepdims=True)) + EPSILON)
    normed = values * factor
    projected = rounded(jnp.dot(normed.astype(jnp.bfloat16), input_weights, preferred_element_type=jnp.float32))
    queries = projected[:, :WIDTH].reshape(nblock, BLOCK, HEADS, HEAD_DIM)
    key_value = projected[:, WIDTH:].reshape(nblock, BLOCK, 2 * WIDTH)
    picked = key_value[key_blocks]
    key_rows = picked[..., :WIDTH].reshape(nblock, slot_count, BLOCK, HEADS, HEAD_DIM)
    value_rows = picked[..., WIDTH:].reshape(nblock, slot_count, BLOCK, HEADS, HEAD_DIM)
    live_slots = (jnp.arange(slot_count)[None, :] < block_counts[:, None])[:, None, None, :, None]
    scores = jnp.einsum('bqhd,bskhd->bhqsk', queries, key_rows, precision=exact) * scaling
    scores = jnp.where(live_slots, scores, -1e+30)
    row_max = lax.optimization_barrier(jnp.max(scores, axis=(3, 4), keepdims=True))
    raw_weights = jnp.where(live_slots, jnp.exp(scores - row_max), 0.0)
    weights = raw_weights / lax.optimization_barrier(jnp.sum(raw_weights, axis=(3, 4), keepdims=True))
    weights_bf = rounded(weights)
    attended = jnp.einsum('bhqsk,bskhd->bqhd', weights_bf, value_rows, precision=exact).reshape(-1, WIDTH).astype(jnp.bfloat16)
    result = (values + jnp.dot(attended, output_weights, preferred_element_type=jnp.float32)).astype(jnp.bfloat16)
    attended_grad = rounded(jnp.dot(upstream, output_weights.T, preferred_element_type=jnp.float32))
    grad_blocks = attended_grad.reshape(nblock, BLOCK, HEADS, HEAD_DIM)
    weight_grad = jnp.einsum('bqhd,bskhd->bhqsk', grad_blocks, value_rows, precision=exact)
    weight_mean = lax.optimization_barrier(jnp.sum(weights * weight_grad, axis=(3, 4), keepdims=True))
    score_grad = rounded(weights * (weight_grad - weight_mean) * scaling)
    query_grad = jnp.einsum('bhqsk,bskhd->bqhd', score_grad, key_rows, precision=exact).reshape(-1, WIDTH)
    key_grad = jnp.einsum('bhqsk,bqhd->bskhd', score_grad, queries, precision=exact).reshape(nblock, slot_count, BLOCK, WIDTH)
    value_grad = jnp.einsum('bhqsk,bqhd->bskhd', weights_bf, grad_blocks, precision=exact).reshape(nblock, slot_count, BLOCK, WIDTH)
    grad_terms = jnp.concatenate([key_grad, value_grad], axis=-1)
    collected = jnp.zeros((nblock, BLOCK, 2 * WIDTH), jnp.float32).at[key_blocks].add(grad_terms)
    all_grads = jnp.concatenate([query_grad, collected.reshape(-1, 2 * WIDTH)], axis=-1).astype(jnp.bfloat16)
    normed_grad = jnp.dot(all_grads, input_weights.T, preferred_element_type=jnp.float32)
    correction = lax.optimization_barrier(jnp.mean(normed_grad * normed, axis=-1, keepdims=True))
    input_grad = (upstream.astype(jnp.float32) + factor * (normed_grad - normed * correction)).astype(jnp.bfloat16)
    return (result, input_grad)

def reference(activations, cotangent, input_weights, output_weights, key_blocks, block_counts):
    outputs = []
    gradients = []
    for section_index in range(N_SECTION):
        result, input_grad = section_layer(activations[(section_index - 1) % N_SECTION], cotangent[(section_index + 1) % N_SECTION], input_weights[section_index], output_weights[section_index], key_blocks, block_counts)
        outputs.append(result)
        gradients.append(input_grad)
    return (jnp.stack(outputs), jnp.stack(gradients))
```

```python
import functools

import jax
import jax.numpy as jnp
from jax import lax
from jax.experimental import pallas as pl
from jax.experimental.pallas import tpu as pltpu
from jax.sharding import PartitionSpec as P

HEAD_DIM = 128
BLOCK = 128
EPSILON = 1e-05
LOG2E = 1.4426950408889634
DEAD = -1e30
MESH = pl.DeviceIdType.MESH

NN = (((1,), (0,)), ((), ()))
NT = (((1,), (1,)), ((), ()))
TN = (((0,), (0,)), ((), ()))


def dot(a, b, dims):
    return lax.dot_general(a, b, dims, preferred_element_type=jnp.float32)


def kernel(
    n_section, n_seq, chunks,
    act, cot, w_in_hbm, w_out_hbm, key_blocks, counts,
    out_fwd, out_bwd,
    w_in, w_out, a_win, c_win, x_bf, qkv, grad_heads, attended, grads, key_grad, value_grad, normed_grad,
    stats, stats_win, w_sems, send_sems, recv_sems, stat_send, stat_recv,
):
    rows, width = act.shape
    heads = width // HEAD_DIM
    scaling = HEAD_DIM ** (-0.5)
    piece = rows // chunks
    slots = key_blocks.shape[1]

    s = lax.axis_index("section")
    q = lax.axis_index("seq")
    odd = lax.rem(q, 2)
    sgn = 1 - 2 * odd
    partner = q + sgn
    far = q - sgn
    z_to = q + 2 * sgn
    z_from = q - 2 * sgn
    has_to = jnp.logical_and(z_to >= 0, z_to < n_seq)
    has_far = jnp.logical_and(z_from >= 0, z_from < n_seq)
    up = lax.rem(s + 1, n_section)
    down = lax.rem(s + n_section - 1, n_section)

    loads = [
        pltpu.make_async_copy(w_in_hbm, w_in, w_sems.at[0]),
        pltpu.make_async_copy(w_out_hbm, w_out, w_sems.at[1]),
    ]
    for load in loads:
        load.start()

    barrier = pltpu.get_barrier_semaphore()

    def greet(section, seq):
        pl.semaphore_signal(barrier, inc=1, device_id=(section, seq), device_id_type=MESH)

    greet(up, q)
    greet(down, q)
    greet(s, partner)

    @pl.when(has_to)
    def _():
        greet(s, z_to)

    @pl.when(has_far)
    def _():
        greet(s, z_from)
        greet(s, far)

    pl.semaphore_wait(barrier, 3 + jnp.where(has_to, 1, 0) + jnp.where(has_far, 2, 0))

    def hop(kind, step, c):
        window = (a_win, c_win)[kind]
        part = pl.ds(c * piece, piece)
        if step == 0:
            src = (act, cot)[kind].at[part]
            target = ((up, down)[kind], q)
        elif step == 1:
            src = window.at[0, part]
            target = (s, partner)
        else:
            src = window.at[1, part]
            target = (s, z_to)
        return pltpu.make_async_remote_copy(
            src_ref=src,
            dst_ref=window.at[step, part],
            send_sem=send_sems.at[kind, step, c],
            recv_sem=recv_sems.at[kind, step, c],
            device_id=target,
            device_id_type=MESH,
        )

    def to_partner(kind, c):
        hop(kind, 0, c).wait_recv()
        hop(kind, 1, c).start()

    def to_far(kind, c):
        hop(kind, 1, c).wait_recv()

        @pl.when(has_to)
        def _():
            hop(kind, 2, c).start()

    for c in range(chunks):
        hop(0, 0, c).start()

    first = q * 2
    starts = (q * 2, partner * 2, far * 2)
    bias = []
    for i in range(2):
        line = []
        for slot in range(3):
            for j in range(2):
                wanted = starts[slot] + j
                found = jnp.float32(DEAD)
                for k in range(slots):
                    hit = jnp.logical_and(key_blocks[i, k] == wanted, counts[i] > k)
                    found = jnp.where(hit, jnp.float32(0.0), found)
                line.append(found)
        bias.append(line)
    lanes = lax.broadcasted_iota(jnp.int32, (1, rows), 1)
    for e in range(6):
        stats[pl.ds(16 + e, 1), :] = jnp.where(lanes < BLOCK, bias[0][e], bias[1][e])

    @pl.when(jnp.logical_not(has_far))
    def _():
        a_win[2] = jnp.zeros((rows, width), jnp.bfloat16)
        c_win[2] = jnp.zeros((rows, width), jnp.bfloat16)
        stats_win[1, 0:16, :] = jnp.zeros((16, rows), jnp.float32)
        stats_win[1, 16:24, :] = jnp.full((8, rows), DEAD, jnp.float32)

    def norm(slot):
        values = a_win[slot].astype(jnp.float32)
        factor = lax.rsqrt(jnp.mean(values * values, axis=-1, keepdims=True) + EPSILON)
        x_bf[...] = (values * factor).astype(jnp.bfloat16)

    tile = 512
    per = tile // HEAD_DIM

    def project(slot, low, high):
        def body(t, carry):
            col = pl.multiple_of(t * tile, tile)
            result = dot(x_bf[...], w_in[:, pl.ds(col, tile)], NN).astype(jnp.bfloat16)
            for i in range(per):
                qkv[t * per + i, slot * rows : (slot + 1) * rows, :] = result[:, i * HEAD_DIM : (i + 1) * HEAD_DIM]
            return carry

        lax.fori_loop(low, high, body, 0)

    def out_grad(slot):
        def body(t, carry):
            row = pl.multiple_of(t * tile, tile)
            result = dot(c_win[slot], w_out[pl.ds(row, tile), :], NT).astype(jnp.bfloat16)
            for i in range(per):
                grad_heads[t * per + i, slot * rows : (slot + 1) * rows, :] = result[:, i * HEAD_DIM : (i + 1) * HEAD_DIM]
            return carry

        lax.fori_loop(0, width // tile, body, 0)

    tiles = 3 * width // tile

    for c in range(chunks):
        to_partner(0, c)
    for c in range(chunks):
        hop(1, 0, c).start()
    norm(0)
    loads[0].wait()
    loads[1].wait()
    for c in range(chunks):
        project(0, tiles * c // chunks, tiles * (c + 1) // chunks)
        to_far(0, c)
    for c in range(chunks):
        to_partner(1, c)
    out_grad(0)
    norm(1)
    project(1, 0, tiles)

    @pl.when(has_far)
    def _():
        for c in range(chunks):
            hop(0, 2, c).wait_recv()

    norm(2)
    project(2, 0, tiles)

    def attend(h, carry):
        query = qkv[h, 0:rows, :]
        keys = qkv[heads + h]
        values = qkv[2 * heads + h]
        grad = grad_heads[h, 0:rows, :]
        raw = dot(keys, query, NT) * (scaling * LOG2E)
        raw = jnp.concatenate(
            [raw[e * BLOCK : (e + 1) * BLOCK] + stats[pl.ds(16 + e, 1), :] for e in range(6)], axis=0
        )
        top = jnp.max(raw, axis=0, keepdims=True)
        power = jnp.exp2(raw - top)
        total = jnp.sum(power, axis=0, keepdims=True)
        weights = power * (1.0 / total)
        weights_bf = weights.astype(jnp.bfloat16)
        column = pl.ds(pl.multiple_of(h * HEAD_DIM, HEAD_DIM), HEAD_DIM)
        attended[:, column] = dot(weights_bf, values, TN).astype(jnp.bfloat16)
        weight_grad = dot(values, grad, NT)
        mean = jnp.sum(weights * weight_grad, axis=0, keepdims=True)
        score_grad = (weights * (weight_grad - mean) * scaling).astype(jnp.bfloat16)
        grads[:, column] = dot(score_grad, keys, TN).astype(jnp.bfloat16)
        key_grad[h] = dot(score_grad[0:rows], query, NN)
        value_grad[h] = dot(weights_bf[0:rows], grad, NN)
        stats[pl.ds(h, 1), :] = top + jnp.log(total) * LOG2E
        stats[pl.ds(heads + h, 1), :] = mean
        return carry

    for c in range(chunks):
        lax.fori_loop(heads * c // chunks, heads * (c + 1) // chunks, attend, 0)
        to_far(1, c)

    def tell(slot):
        return pltpu.make_async_remote_copy(
            src_ref=stats,
            dst_ref=stats_win.at[slot - 1],
            send_sem=stat_send.at[slot - 1],
            recv_sem=stat_recv.at[slot - 1],
            device_id=(s, partner if slot == 1 else far),
            device_id_type=MESH,
        )

    tell(1).start()

    @pl.when(has_far)
    def _():
        tell(2).start()

    def forward(t, carry):
        column = pl.ds(pl.multiple_of(t * tile, tile), tile)
        result = dot(attended[...], w_out[:, column], NN)
        out_fwd[:, column] = (a_win[0, :, column].astype(jnp.float32) + result).astype(jnp.bfloat16)
        return carry

    lax.fori_loop(0, width // tile, forward, 0)

    def backward(part):
        def body(t, carry):
            there = pl.ds(pl.multiple_of(t * tile, tile), tile)
            term = dot(grads[:, part * width : (part + 1) * width], w_in[there, part * width : (part + 1) * width], NT)
            if part == 0:
                normed_grad[:, there] = term
            else:
                normed_grad[:, there] += term
            return carry

        lax.fori_loop(0, width // tile, body, 0)

    backward(0)

    def collect(slot):
        def body(h, carry):
            here = slice(slot * rows, (slot + 1) * rows)
            query = qkv[h, here, :]
            keys = qkv[heads + h, 0:rows, :]
            values = qkv[2 * heads + h, 0:rows, :]
            grad = grad_heads[h, here, :]
            level = stats_win[slot - 1, pl.ds(h, 1), :]
            mean = stats_win[slot - 1, pl.ds(heads + h, 1), :]
            raw = dot(keys, query, NT) * (scaling * LOG2E)
            weights = jnp.concatenate(
                [
                    jnp.exp2(raw[e * BLOCK : (e + 1) * BLOCK] + (stats_win[slot - 1, pl.ds(16 + 2 * slot + e, 1), :] - level))
                    for e in range(2)
                ],
                axis=0,
            )
            weight_grad = dot(values, grad, NT)
            score_grad = (weights * (weight_grad - mean) * scaling).astype(jnp.bfloat16)
            key_sum = key_grad[h] + dot(score_grad, query, NN)
            value_sum = value_grad[h] + dot(weights.astype(jnp.bfloat16), grad, NN)
            if slot == 1:
                key_grad[h] = key_sum
                value_grad[h] = value_sum
            else:
                grads[:, pl.ds(pl.multiple_of(width + h * HEAD_DIM, HEAD_DIM), HEAD_DIM)] = key_sum.astype(jnp.bfloat16)
                grads[:, pl.ds(pl.multiple_of(2 * width + h * HEAD_DIM, HEAD_DIM), HEAD_DIM)] = value_sum.astype(jnp.bfloat16)
            return carry

        lax.fori_loop(0, heads, body, 0)

    out_grad(1)
    tell(1).wait_recv()
    collect(1)

    @pl.when(has_far)
    def _():
        for c in range(chunks):
            hop(1, 2, c).wait_recv()
        tell(2).wait_recv()

    out_grad(2)
    collect(2)
    backward(1)
    backward(2)

    values = a_win[0].astype(jnp.float32)
    factor = lax.rsqrt(jnp.mean(values * values, axis=-1, keepdims=True) + EPSILON)
    normed = values * factor
    total_grad = normed_grad[...]
    correction = jnp.mean(total_grad * normed, axis=-1, keepdims=True)
    out_bwd[...] = (c_win[0].astype(jnp.float32) + factor * (total_grad - normed * correction)).astype(jnp.bfloat16)

    for kind in range(2):
        for c in range(chunks):
            hop(kind, 0, c).wait_send()
            hop(kind, 1, c).wait_send()
    tell(1).wait_send()

    @pl.when(has_to)
    def _():
        for kind in range(2):
            for c in range(chunks):
                hop(kind, 2, c).wait_send()

    @pl.when(has_far)
    def _():
        tell(2).wait_send()


def per_device(n_section, n_seq, activations, cotangent, input_weights, output_weights, key_blocks, block_counts):
    act, cot, w_in, w_out = activations[0], cotangent[0], input_weights[0], output_weights[0]
    rows, width = act.shape
    heads = width // HEAD_DIM
    chunks = 4
    bf, f32 = jnp.bfloat16, jnp.float32
    hbm = pl.BlockSpec(memory_space=pl.ANY)
    smem = pl.BlockSpec(memory_space=pltpu.SMEM)
    vmem = pl.BlockSpec(memory_space=pltpu.VMEM)
    fwd, bwd = pl.pallas_call(
        functools.partial(kernel, n_section, n_seq, chunks),
        out_shape=[jax.ShapeDtypeStruct((rows, width), bf)] * 2,
        in_specs=[hbm] * 4 + [smem] * 2,
        out_specs=[vmem] * 2,
        scratch_shapes=[
            pltpu.VMEM((width, 3 * width), bf),
            pltpu.VMEM((width, width), bf),
            pltpu.VMEM((3, rows, width), bf),
            pltpu.VMEM((3, rows, width), bf),
            pltpu.VMEM((rows, width), bf),
            pltpu.VMEM((3 * heads, 3 * rows, HEAD_DIM), bf),
            pltpu.VMEM((heads, 3 * rows, HEAD_DIM), bf),
            pltpu.VMEM((rows, width), bf),
            pltpu.VMEM((rows, 3 * width), bf),
            pltpu.VMEM((heads, rows, HEAD_DIM), f32),
            pltpu.VMEM((heads, rows, HEAD_DIM), f32),
            pltpu.VMEM((rows, width), f32),
            pltpu.VMEM((24, rows), f32),
            pltpu.VMEM((2, 24, rows), f32),
            pltpu.SemaphoreType.DMA((2,)),
            pltpu.SemaphoreType.DMA((2, 3, chunks)),
            pltpu.SemaphoreType.DMA((2, 3, chunks)),
            pltpu.SemaphoreType.DMA((2,)),
            pltpu.SemaphoreType.DMA((2,)),
        ],
        compiler_params=pltpu.CompilerParams(
            collective_id=0, has_side_effects=True, vmem_limit_bytes=56 * 2**20
        ),
    )(act, cot, w_in, w_out, key_blocks, block_counts)
    return fwd[None], bwd[None]


def solution(mesh):
    in_specs = (
        P("section", "seq", None),
        P("section", "seq", None),
        P("section", None, None),
        P("section", None, None),
        P("seq", None),
        P("seq"),
    )
    out_specs = (P("section", "seq", None), P("section", "seq", None))
    return jax.shard_map(
        functools.partial(per_device, mesh.shape["section"], mesh.shape["seq"]),
        mesh=mesh, in_specs=in_specs, out_specs=out_specs, check_vma=False,
    )
```

```python
import functools

import jax
import jax.numpy as jnp
from jax import lax
from jax.experimental import pallas as pl
from jax.experimental.pallas import tpu as pltpu
from jax.sharding import PartitionSpec as P

HEAD_DIM = 128
BLOCK = 128
EPSILON = 1e-05
LOG2E = 1.4426950408889634
DEAD = -1e30
MESH = pl.DeviceIdType.MESH

NN = (((1,), (0,)), ((), ()))
NT = (((1,), (1,)), ((), ()))
TN = (((0,), (0,)), ((), ()))


def dot(a, b, dims):
    return lax.dot_general(a, b, dims, preferred_element_type=jnp.float32)


def kernel(
    n_section, n_seq, chunks,
    act, cot, w_in_hbm, w_out_hbm, key_blocks, counts,
    out_fwd, out_bwd,
    w_in, w_out, a_win, c_win, x_bf, qkv, grad_heads, attended, grads, key_grad, value_grad, normed_grad,
    stats, stats_win, w_sems, send_sems, recv_sems, stat_send, stat_recv,
):
    rows, width = act.shape
    heads = width // HEAD_DIM
    scaling = HEAD_DIM ** (-0.5)
    piece = rows // chunks
    slots = key_blocks.shape[1]

    s = lax.axis_index("section")
    q = lax.axis_index("seq")
    odd = lax.rem(q, 2)
    sgn = 1 - 2 * odd
    partner = q + sgn
    far = q - sgn
    z_to = q + 2 * sgn
    z_from = q - 2 * sgn
    has_to = jnp.logical_and(z_to >= 0, z_to < n_seq)
    has_far = jnp.logical_and(z_from >= 0, z_from < n_seq)
    up = lax.rem(s + 1, n_section)
    down = lax.rem(s + n_section - 1, n_section)

    loads = [
        pltpu.make_async_copy(w_in_hbm, w_in, w_sems.at[0]),
        pltpu.make_async_copy(w_out_hbm, w_out, w_sems.at[1]),
    ]
    for load in loads:
        load.start()

    barrier = pltpu.get_barrier_semaphore()

    def greet(section, seq):
        pl.semaphore_signal(barrier, inc=1, device_id=(section, seq), device_id_type=MESH)

    greet(up, q)
    greet(down, q)
    greet(s, partner)

    @pl.when(has_to)
    def _():
        greet(s, z_to)

    @pl.when(has_far)
    def _():
        greet(s, z_from)
        greet(s, far)

    pl.semaphore_wait(barrier, 3 + jnp.where(has_to, 1, 0) + jnp.where(has_far, 2, 0))

    def hop(kind, step, c):
        window = (a_win, c_win)[kind]
        part = pl.ds(c * piece, piece)
        if step == 0:
            src = (act, cot)[kind].at[part]
            target = ((up, down)[kind], q)
        elif step == 1:
            src = window.at[0, part]
            target = (s, partner)
        else:
            src = window.at[1, part]
            target = (s, z_to)
        return pltpu.make_async_remote_copy(
            src_ref=src,
            dst_ref=window.at[step, part],
            send_sem=send_sems.at[kind, step, c],
            recv_sem=recv_sems.at[kind, step, c],
            device_id=target,
            device_id_type=MESH,
        )

    def to_partner(kind, c):
        hop(kind, 0, c).wait_recv()
        hop(kind, 1, c).start()

    def to_far(kind, c):
        hop(kind, 1, c).wait_recv()

        @pl.when(has_to)
        def _():
            hop(kind, 2, c).start()

    for c in range(chunks):
        hop(0, 0, c).start()

    first = q * 2
    starts = (q * 2, partner * 2, far * 2)
    bias = []
    for i in range(2):
        line = []
        for slot in range(3):
            for j in range(2):
                wanted = starts[slot] + j
                found = jnp.float32(DEAD)
                for k in range(slots):
                    hit = jnp.logical_and(key_blocks[i, k] == wanted, counts[i] > k)
                    found = jnp.where(hit, jnp.float32(0.0), found)
                line.append(found)
        bias.append(line)
    lanes = lax.broadcasted_iota(jnp.int32, (1, rows), 1)
    for e in range(6):
        stats[pl.ds(16 + e, 1), :] = jnp.where(lanes < BLOCK, bias[0][e], bias[1][e])

    @pl.when(jnp.logical_not(has_far))
    def _():
        a_win[2] = jnp.zeros((rows, width), jnp.bfloat16)
        c_win[2] = jnp.zeros((rows, width), jnp.bfloat16)
        stats_win[1, 0:16, :] = jnp.zeros((16, rows), jnp.float32)
        stats_win[1, 16:24, :] = jnp.full((8, rows), DEAD, jnp.float32)

    def norm(slot, top, size):
        values = a_win[slot, top : top + size].astype(jnp.float32)
        factor = lax.rsqrt(jnp.mean(values * values, axis=-1, keepdims=True) + EPSILON)
        x_bf[top : top + size] = (values * factor).astype(jnp.bfloat16)

    tile = 512
    per = tile // HEAD_DIM

    def project(slot, top, size, low, high):
        for t in range(low, high):
            result = dot(x_bf[top : top + size], w_in[:, t * tile : (t + 1) * tile], NN).astype(jnp.bfloat16)
            for i in range(per):
                qkv[t * per + i, slot * rows + top : slot * rows + top + size, :] = result[:, i * HEAD_DIM : (i + 1) * HEAD_DIM]

    def out_grad(slot):
        def body(t, carry):
            row = pl.multiple_of(t * tile, tile)
            result = dot(c_win[slot], w_out[pl.ds(row, tile), :], NT).astype(jnp.bfloat16)
            for i in range(per):
                grad_heads[t * per + i, slot * rows : (slot + 1) * rows, :] = result[:, i * HEAD_DIM : (i + 1) * HEAD_DIM]
            return carry

        lax.fori_loop(0, width // tile, body, 0, unroll=True)

    tiles = 3 * width // tile

    def far_arrived(c):
        @pl.when(has_far)
        def _():
            hop(0, 2, c).wait_recv()

    for c in range(chunks):
        to_partner(0, c)
    for c in range(chunks):
        hop(1, 0, c).start()
    norm(0, 0, rows)
    loads[0].wait()
    loads[1].wait()
    project(0, 0, rows, 0, tiles // 2)
    to_far(0, 0)
    project(0, 0, rows, tiles // 2, tiles)
    to_far(0, 1)
    half = rows // 2
    norm(1, 0, half)
    project(1, 0, half, 0, tiles)
    to_far(0, 2)
    far_arrived(0)
    far_arrived(1)
    norm(2, 0, half)
    project(2, 0, half, 0, tiles)
    to_far(0, 3)
    to_partner(1, 0)
    to_partner(1, 1)
    norm(1, half, half)
    project(1, half, half, 0, tiles)
    to_partner(1, 2)
    to_partner(1, 3)
    out_grad(0)
    far_arrived(2)
    far_arrived(3)
    norm(2, half, half)
    project(2, half, half, 0, tiles)

    def attend(h, carry):
        query = qkv[h, 0:rows, :]
        keys = qkv[heads + h]
        values = qkv[2 * heads + h]
        grad = grad_heads[h, 0:rows, :]
        raw = dot(keys, query, NT) * (scaling * LOG2E)
        raw = jnp.concatenate(
            [raw[e * BLOCK : (e + 1) * BLOCK] + stats[pl.ds(16 + e, 1), :] for e in range(6)], axis=0
        )
        top = jnp.max(raw, axis=0, keepdims=True)
        power = jnp.exp2(raw - top)
        total = jnp.sum(power, axis=0, keepdims=True)
        weights = power * (1.0 / total)
        weights_bf = weights.astype(jnp.bfloat16)
        column = pl.ds(pl.multiple_of(h * HEAD_DIM, HEAD_DIM), HEAD_DIM)
        attended[:, column] = dot(weights_bf, values, TN).astype(jnp.bfloat16)
        weight_grad = dot(values, grad, NT)
        mean = jnp.sum(weights * weight_grad, axis=0, keepdims=True)
        score_grad = (weights * (weight_grad - mean) * scaling).astype(jnp.bfloat16)
        grads[:, column] = dot(score_grad, keys, TN).astype(jnp.bfloat16)
        key_grad[h] = dot(score_grad[0:rows], query, NN)
        value_grad[h] = dot(weights_bf[0:rows], grad, NN)
        stats[pl.ds(h, 1), :] = top + jnp.log(total) * LOG2E
        stats[pl.ds(heads + h, 1), :] = mean
        return carry

    for c in range(chunks):
        lax.fori_loop(heads * c // chunks, heads * (c + 1) // chunks, attend, 0, unroll=2)
        to_far(1, c)

    def tell(slot):
        return pltpu.make_async_remote_copy(
            src_ref=stats,
            dst_ref=stats_win.at[slot - 1],
            send_sem=stat_send.at[slot - 1],
            recv_sem=stat_recv.at[slot - 1],
            device_id=(s, partner if slot == 1 else far),
            device_id_type=MESH,
        )

    tell(1).start()

    @pl.when(has_far)
    def _():
        tell(2).start()

    def forward(t, carry):
        column = pl.ds(pl.multiple_of(t * tile, tile), tile)
        result = dot(attended[...], w_out[:, column], NN)
        out_fwd[:, column] = (a_win[0, :, column].astype(jnp.float32) + result).astype(jnp.bfloat16)
        return carry

    lax.fori_loop(0, width // tile, forward, 0, unroll=True)

    def backward(part):
        def body(t, carry):
            there = pl.ds(pl.multiple_of(t * tile, tile), tile)
            term = dot(grads[:, part * width : (part + 1) * width], w_in[there, part * width : (part + 1) * width], NT)
            if part == 0:
                normed_grad[:, there] = term
            else:
                normed_grad[:, there] += term
            return carry

        lax.fori_loop(0, width // tile, body, 0, unroll=True)

    backward(0)

    def collect(slot):
        def body(h, carry):
            here = slice(slot * rows, (slot + 1) * rows)
            query = qkv[h, here, :]
            keys = qkv[heads + h, 0:rows, :]
            values = qkv[2 * heads + h, 0:rows, :]
            grad = grad_heads[h, here, :]
            level = stats_win[slot - 1, pl.ds(h, 1), :]
            mean = stats_win[slot - 1, pl.ds(heads + h, 1), :]
            raw = dot(keys, query, NT) * (scaling * LOG2E)
            weights = jnp.concatenate(
                [
                    jnp.exp2(raw[e * BLOCK : (e + 1) * BLOCK] + (stats_win[slot - 1, pl.ds(16 + 2 * slot + e, 1), :] - level))
                    for e in range(2)
                ],
                axis=0,
            )
            weight_grad = dot(values, grad, NT)
            score_grad = (weights * (weight_grad - mean) * scaling).astype(jnp.bfloat16)
            key_sum = key_grad[h] + dot(score_grad, query, NN)
            value_sum = value_grad[h] + dot(weights.astype(jnp.bfloat16), grad, NN)
            if slot == 1:
                key_grad[h] = key_sum
                value_grad[h] = value_sum
            else:
                grads[:, pl.ds(pl.multiple_of(width + h * HEAD_DIM, HEAD_DIM), HEAD_DIM)] = key_sum.astype(jnp.bfloat16)
                grads[:, pl.ds(pl.multiple_of(2 * width + h * HEAD_DIM, HEAD_DIM), HEAD_DIM)] = value_sum.astype(jnp.bfloat16)
            return carry

        lax.fori_loop(0, heads, body, 0, unroll=4)

    out_grad(1)
    tell(1).wait_recv()
    collect(1)

    @pl.when(has_far)
    def _():
        for c in range(chunks):
            hop(1, 2, c).wait_recv()
        tell(2).wait_recv()

    out_grad(2)
    collect(2)
    backward(1)
    backward(2)

    values = a_win[0].astype(jnp.float32)
    factor = lax.rsqrt(jnp.mean(values * values, axis=-1, keepdims=True) + EPSILON)
    normed = values * factor
    total_grad = normed_grad[...]
    correction = jnp.mean(total_grad * normed, axis=-1, keepdims=True)
    out_bwd[...] = (c_win[0].astype(jnp.float32) + factor * (total_grad - normed * correction)).astype(jnp.bfloat16)

    for kind in range(2):
        for c in range(chunks):
            hop(kind, 0, c).wait_send()
            hop(kind, 1, c).wait_send()
    tell(1).wait_send()

    @pl.when(has_to)
    def _():
        for kind in range(2):
            for c in range(chunks):
                hop(kind, 2, c).wait_send()

    @pl.when(has_far)
    def _():
        tell(2).wait_send()


def per_device(n_section, n_seq, activations, cotangent, input_weights, output_weights, key_blocks, block_counts):
    act, cot, w_in, w_out = activations[0], cotangent[0], input_weights[0], output_weights[0]
    rows, width = act.shape
    heads = width // HEAD_DIM
    chunks = 4
    bf, f32 = jnp.bfloat16, jnp.float32
    hbm = pl.BlockSpec(memory_space=pl.ANY)
    smem = pl.BlockSpec(memory_space=pltpu.SMEM)
    vmem = pl.BlockSpec(memory_space=pltpu.VMEM)
    fwd, bwd = pl.pallas_call(
        functools.partial(kernel, n_section, n_seq, chunks),
        out_shape=[jax.ShapeDtypeStruct((rows, width), bf)] * 2,
        in_specs=[hbm] * 4 + [smem] * 2,
        out_specs=[vmem] * 2,
        scratch_shapes=[
            pltpu.VMEM((width, 3 * width), bf),
            pltpu.VMEM((width, width), bf),
            pltpu.VMEM((3, rows, width), bf),
            pltpu.VMEM((3, rows, width), bf),
            pltpu.VMEM((rows, width), bf),
            pltpu.VMEM((3 * heads, 3 * rows, HEAD_DIM), bf),
            pltpu.VMEM((heads, 3 * rows, HEAD_DIM), bf),
            pltpu.VMEM((rows, width), bf),
            pltpu.VMEM((rows, 3 * width), bf),
            pltpu.VMEM((heads, rows, HEAD_DIM), f32),
            pltpu.VMEM((heads, rows, HEAD_DIM), f32),
            pltpu.VMEM((rows, width), f32),
            pltpu.VMEM((24, rows), f32),
            pltpu.VMEM((2, 24, rows), f32),
            pltpu.SemaphoreType.DMA((2,)),
            pltpu.SemaphoreType.DMA((2, 3, chunks)),
            pltpu.SemaphoreType.DMA((2, 3, chunks)),
            pltpu.SemaphoreType.DMA((2,)),
            pltpu.SemaphoreType.DMA((2,)),
        ],
        compiler_params=pltpu.CompilerParams(
            collective_id=0, has_side_effects=True, vmem_limit_bytes=56 * 2**20
        ),
    )(act, cot, w_in, w_out, key_blocks, block_counts)
    return fwd[None], bwd[None]


def solution(mesh):
    in_specs = (
        P("section", "seq", None),
        P("section", "seq", None),
        P("section", None, None),
        P("section", None, None),
        P("seq", None),
        P("seq"),
    )
    out_specs = (P("section", "seq", None), P("section", "seq", None))
    return jax.shard_map(
        functools.partial(per_device, mesh.shape["section"], mesh.shape["seq"]),
        mesh=mesh, in_specs=in_specs, out_specs=out_specs, check_vma=False,
    )
```
